128 devices in a mesh: expert: 64 (over z, x, y_lo, core), dp: 2 (over y_hi).
Axes of the slice: x: 4, y: 4 (y_hi: 2, y_lo: 2; y = y_hi * 2 + y_lo), z: 4, core: 2. Of those that a mesh axis runs over, the one named last changes fastest.
Arguments:
- tokens: bfloat16 [2, 32768, 1024], P('dp', 'expert'), may hold values from -6 to 6
- cotangent: bfloat16 [2, 32768, 1024], P('dp', 'expert'), may hold values from -6 to 6
- assign: int32 [2, 32768], P('dp', 'expert'), may hold values from 0 to 32767, as said below
- gain: float32 [64, 1024], P('expert'), may hold values from 0.1 to 1.9
- router: bfloat16 [64, 1024], P('expert'), may hold values from -0.1875 to 0.1875
- w_in: bfloat16 [64, 2048, 1024], P('expert', 'dp'), may hold values from -0.1875 to 0.1875
- w_out: bfloat16 [64, 2048, 1024], P('expert', 'dp'), may hold values from -0.125 to 0.125
Outputs:
- mixed: bfloat16 [2, 32768, 1024], P('dp', 'expert')
- input_grad: bfloat16 [2, 32768, 1024], P('dp', 'expert')
- w_in_grad: float32 [64, 2048, 1024], P('expert', 'dp')
- w_out_grad: float32 [64, 2048, 1024], P('expert', 'dp')
- gain_grad: float32 [64, 1024], P('expert')
- router_grad: float32 [64, 1024], P('expert')
The draws below stay inside these ranges and needn't reach their ends.
Inputs may be any that keep to these rules, and one draw needn't show every extreme that they name: Each row of assign is a permutation of the 32768 slots, so every expert receives 512 tokens of each group. Of the 512 tokens of one device, at most 16 go to one expert, and in every draw each device sends exactly 16 to some expert.
All inputs are finite; a program needn't handle non-finite values.
Results may differ from the reference program's by a relative error of at most 0.0062.
Values may be sent and summed in bfloat16 or wider, within the bound.
No kernel may reach another device: no remote copies, remote signals or barrier semaphores. Data moves between devices by JAX's collectives and lax.ppermute only.
A program may use at most 192 MiB of HBM per device.

```python
import jax
import jax.numpy as jnp
from jax import lax

D = 1024
H = 2048
TOK_DEV = 512
EXPERTS = 64
TOK_GROUP = 32768
N_EXPERT = 64
N_DP = 2


def group_assign(key):
    experts = N_EXPERT
    base = TOK_DEV // N_EXPERT
    half = experts // 2
    k_delta, k_pick, k_order, k_label, k_local = jax.random.split(key, 5)
    delta = jax.random.randint(k_delta, (half,), -(base - 1), base + 1)
    delta = delta.at[jax.random.randint(k_pick, (), 0, half)].set(base)
    counts = jnp.stack([base + delta, base - delta], 1).reshape(experts).astype(jnp.int32)
    counts = counts[jax.random.permutation(k_order, experts)]
    relabel = jax.random.permutation(k_label, experts)
    source = jnp.arange(experts, dtype=jnp.int32)
    target_of = relabel[(source[:, None] + source[None, :]) % experts]
    matrix = jnp.zeros((experts, experts), jnp.int32).at[source[:, None], target_of].set(jnp.broadcast_to(counts[None, :], (experts, experts)))
    inclusive = jnp.cumsum(matrix, 1)
    earlier = jnp.cumsum(matrix, 0) - matrix
    ranks = jnp.arange(TOK_DEV, dtype=jnp.int32)
    target = jnp.sum((inclusive[:, None, :] <= ranks[None, :, None]).astype(jnp.int32), 2)
    within = ranks[None, :] - jnp.take_along_axis(inclusive - matrix, target, 1)
    slot = target * TOK_DEV + jnp.take_along_axis(earlier, target, 1) + within
    order = jax.vmap(lambda k: jax.random.permutation(k, TOK_DEV))(jax.random.split(k_local, experts))
    placed = jnp.zeros((experts, TOK_DEV), jnp.int32).at[source[:, None], order].set(slot)
    return placed.reshape(experts * TOK_DEV)


def draw_assign(key, part):
    key = jax.random.fold_in(key, 11)
    return jax.vmap(group_assign)(jax.random.split(key, N_DP)).astype(jnp.int32)


def shard_levels(own_key, dims, shards, least, top_value):
    loudness, own = 1.0, jax.random.fold_in(own_key, 6)
    for dim, shards_of in shards:
        steps = jnp.exp(jax.random.uniform(jax.random.fold_in(own, dim), (shards_of,), jnp.float32, least / len(shards), top_value / len(shards)))
        loudness = loudness * jnp.repeat(steps, dims[dim] // shards_of).reshape([-1 if axis == dim else 1 for axis in range(len(dims))])
    return loudness


def gaussian(stream_key, extent, spread, reach, cuts=(), kind=jnp.bfloat16):
    array = spread * jax.random.normal(stream_key, extent, jnp.float32)
    if cuts:
        array = array * shard_levels(stream_key, extent, cuts, -0.22, 0.18)
    return jnp.clip(array, -reach, reach).astype(kind)


def setup_inputs(seed: int = 0) -> dict:
    key_of = jax.random.split(jax.random.key(seed), 8)
    return {
        "tokens": gaussian(key_of[0], (N_DP, TOK_GROUP, D), 1.0, 6.0, ((0, 2), (1, 64))),
        "cotangent": gaussian(key_of[1], (N_DP, TOK_GROUP, D), 1.0, 6.0, ((0, 2), (1, 64))),
        "assign": draw_assign(jax.random.fold_in(key_of[7], 71), 0),
        "gain": jnp.clip(1.0 + 0.18 * jax.random.normal(key_of[3], (EXPERTS, D), jnp.float32), 0.1, 1.9),
        "router": gaussian(key_of[4], (EXPERTS, D), D ** -0.5, 0.1875, ((0, 64),)),
        "w_in": gaussian(key_of[5], (EXPERTS, H, D), D ** -0.5, 0.1875, ((0, 64), (1, 2))),
        "w_out": gaussian(key_of[6], (EXPERTS, H, D), H ** -0.5, 0.125, ((0, 64), (1, 2))),
    }


EPS = 1e-05

def gelu_fn(values):
    return jax.nn.gelu(values, approximate=True)

def expert_pass(args):
    rows, cot_rows, gain_row, router_row, w_in_one, w_out_one = args
    xf = rows.astype(jnp.float32)
    inv = lax.rsqrt(lax.optimization_barrier(jnp.mean(xf * xf, -1, keepdims=True)) + EPS)
    unit = xf * inv
    normed = (unit * gain_row).astype(jnp.bfloat16)
    gate = jax.nn.sigmoid(jnp.dot(rows, router_row, preferred_element_type=jnp.float32))[:, None]
    pre = jnp.dot(normed, w_in_one.T, preferred_element_type=jnp.float32)
    hid = gelu_fn(pre).astype(jnp.bfloat16)
    branch = jnp.dot(hid, w_out_one, preferred_element_type=jnp.float32)
    mixed = (xf + gate * branch).astype(jnp.bfloat16)
    dyf = cot_rows.astype(jnp.float32)
    dlogit = lax.optimization_barrier(jnp.sum(dyf * branch, -1, keepdims=True)) * gate * (1.0 - gate)
    dbranch = (gate * dyf).astype(jnp.bfloat16)
    dhid = jnp.dot(dbranch, w_out_one.T, preferred_element_type=jnp.float32)
    pull = jax.vjp(gelu_fn, pre)[1]
    dpre = pull(dhid)[0].astype(jnp.bfloat16)
    dnormed = jnp.dot(dpre, w_in_one, preferred_element_type=jnp.float32)
    dunit = dnormed * gain_row
    back = dyf + inv * (dunit - unit * lax.optimization_barrier(jnp.mean(dunit * unit, -1, keepdims=True))) + dlogit * router_row.astype(jnp.float32)
    grad_in = lax.dot_general(dpre, normed, (((0,), (0,)), ((), ())), preferred_element_type=jnp.float32)
    grad_out = lax.dot_general(hid, dbranch, (((0,), (0,)), ((), ())), preferred_element_type=jnp.float32)
    gain_part = lax.optimization_barrier(jnp.sum(dnormed * unit, 0))
    router_part = lax.optimization_barrier(jnp.sum(dlogit * xf, 0))
    return (mixed, back.astype(jnp.bfloat16), grad_in, grad_out, gain_part, router_part)

def reference(tokens, cotangent, assign, gain, router, w_in, w_out):

    def place(values):
        stacked = jnp.stack([jnp.zeros((TOK_GROUP, D), values.dtype).at[assign[g]].set(values[g]) for g in range(N_DP)], 0)
        return stacked.reshape(N_DP, N_EXPERT, TOK_DEV, D).transpose(1, 0, 2, 3).reshape(N_EXPERT, N_DP * TOK_DEV, D)
    mixed_e, back_e, grad_in, grad_out, gain_grad, router_grad = lax.map(expert_pass, (place(tokens), place(cotangent), gain, router, w_in, w_out))

    def home(values):
        grouped = values.reshape(N_EXPERT, N_DP, TOK_DEV, D).transpose(1, 0, 2, 3).reshape(N_DP, TOK_GROUP, D)
        return jnp.stack([grouped[g][assign[g]] for g in range(N_DP)], 0)
    return (home(mixed_e), home(back_e), grad_in, grad_out, gain_grad, router_grad)
```

```python
import jax
import jax.numpy as jnp
from jax import lax
from jax.sharding import PartitionSpec as P

EPS = 1e-05
FILL = 64.0
SWAP = ((0, 1), (1, 0))


def gelu_fn(values):
    return jax.nn.gelu(values, approximate=True)


def dot(left, right, dims):
    return lax.dot_general(left, right, (dims, ((), ())), preferred_element_type=jnp.float32)


def swap(values):
    return lax.ppermute(values, "dp", SWAP)


def exchange(buffer, experts):
    rows, width = buffer.shape
    out = lax.all_to_all(
        buffer.reshape(experts, rows // experts, width), "expert", split_axis=0, concat_axis=0, tiled=True
    )
    return out.reshape(rows, width)


def normalize(rows, gain_row):
    xf = rows.astype(jnp.float32)
    inv = lax.rsqrt(jnp.mean(xf * xf, -1, keepdims=True) + EPS)
    unit = xf * inv
    return inv, unit, (unit * gain_row).astype(jnp.bfloat16)


def gate_of(rows, router_row):
    return jax.nn.sigmoid(jnp.dot(rows, router_row, preferred_element_type=jnp.float32))[:, None]


def local(tokens, cotangent, assign, gain, router, w_in, w_out):
    experts = lax.axis_size("expert")
    tok = tokens.shape[1]
    cap = 2 * tok // experts
    slots = experts * cap
    bf = jnp.bfloat16
    target = assign[0] // tok
    onehot = (target[:, None] == jnp.arange(experts, dtype=jnp.int32)[None, :]).astype(jnp.int32)
    rank = jnp.sum((jnp.cumsum(onehot, 0) - onehot) * onehot, 1)
    where = target * cap + rank
    place = (where[:, None] == jnp.arange(slots, dtype=jnp.int32)[None, :]).astype(bf)
    empty = 1.0 - jnp.sum(place.astype(jnp.float32), 0)

    gain_row, router_row = gain[0], router[0]
    win, wout = w_in[0], w_out[0]

    x_pack = (dot(place, tokens[0], ((0,), (0,))) + FILL * empty[:, None]).astype(bf)
    dy_pack = dot(place, cotangent[0], ((0,), (0,))).astype(bf)
    x_buf = exchange(x_pack, experts)
    valid = x_buf[:, 0] < 0.5 * FILL
    pos = jnp.where(valid, jnp.cumsum(valid.astype(jnp.int32)) - 1, -1)
    pick = (pos[None, :] == jnp.arange(tok, dtype=jnp.int32)[:, None]).astype(bf)
    x_own = dot(pick, x_buf, ((1,), (0,))).astype(bf)
    x_peer = swap(x_own)
    dy_buf = exchange(dy_pack, experts)
    dy_own = dot(pick, dy_buf, ((1,), (0,)))
    inv_o, unit_o, normed_o = normalize(x_own, gain_row)
    gate_o = gate_of(x_own, router_row)
    pre_o = dot(normed_o, win, ((1,), (1,)))
    hid_o = gelu_fn(pre_o).astype(bf)
    part_o = dot(hid_o, wout, ((1,), (0,)))
    db_o = (gate_o * dy_own).astype(bf)
    db_p = swap(db_o)

    inv_p, unit_p, normed_p = normalize(x_peer, gain_row)
    pre_p = dot(normed_p, win, ((1,), (1,)))
    hid_p = gelu_fn(pre_p).astype(bf)
    part_p = dot(hid_p, wout, ((1,), (0,))).astype(bf)
    branch = part_o + swap(part_p).astype(jnp.float32)

    def backward(pre, db):
        dhid = dot(db, wout, ((1,), (1,)))
        dpre = jax.vjp(gelu_fn, pre)[1](dhid)[0].astype(bf)
        return dpre, dot(dpre, win, ((1,), (0,)))

    dpre_p, dn_p = backward(pre_p, db_p)
    dn_recv = swap(dn_p.astype(bf))
    dpre_o, dn_o = backward(pre_o, db_o)
    grad_in = dot(dpre_o, normed_o, ((0,), (0,))) + dot(dpre_p, normed_p, ((0,), (0,)))
    grad_out = dot(hid_o, db_o, ((0,), (0,))) + dot(hid_p, db_p, ((0,), (0,)))
    gain_part = jnp.sum(dn_o * unit_o, 0) + jnp.sum(dn_p * unit_p, 0)

    xf = x_own.astype(jnp.float32)
    y_rows = (xf + gate_o * branch).astype(bf)
    y_buf = exchange(dot(pick, y_rows, ((0,), (0,))).astype(bf), experts)
    dlogit = jnp.sum(dy_own * branch, -1, keepdims=True) * gate_o * (1.0 - gate_o)
    router_part = jnp.sum(dlogit * xf, 0)
    small = jnp.stack([gain_part, router_part])
    small = small + swap(small)

    dunit = (dn_o + dn_recv.astype(jnp.float32)) * gain_row
    back = (
        dy_own
        + inv_o * (dunit - unit_o * jnp.mean(dunit * unit_o, -1, keepdims=True))
        + dlogit * router_row.astype(jnp.float32)
    ).astype(bf)
    back_buf = exchange(dot(pick, back, ((0,), (0,))).astype(bf), experts)
    mixed = dot(place, y_buf, ((1,), (0,))).astype(bf)
    input_grad = dot(place, back_buf, ((1,), (0,))).astype(bf)
    return (mixed[None], input_grad[None], grad_in[None], grad_out[None], small[:1], small[1:])


def solution(mesh):
    return jax.shard_map(
        local,
        mesh=mesh,
        in_specs=(
            P("dp", "expert", None),
            P("dp", "expert", None),
            P("dp", "expert"),
            P("expert", None),
            P("expert", None),
            P("expert", "dp", None),
            P("expert", "dp", None),
        ),
        out_specs=(
            P("dp", "expert", None),
            P("dp", "expert", None),
            P("expert", "dp", None),
            P("expert", "dp", None),
            P("expert", None),
            P("expert", None),
        ),
        check_vma=False,
    )
```

```python
import functools

import jax
import jax.numpy as jnp
from jax import lax
from jax.experimental import pallas as pl
from jax.experimental.pallas import tpu as pltpu
from jax.sharding import PartitionSpec as P

EPS = 1e-05
FILL = 64.0
SWAP = ((0, 1), (1, 0))
BF = jnp.bfloat16
F32 = jnp.float32
MIB = 1024 * 1024
TAIL = 16
GF = 10**12


def dot(left, right, dims):
    return lax.dot_general(left, right, (dims, ((), ())), preferred_element_type=F32)


def iota(shape, dim):
    return lax.broadcasted_iota(jnp.int32, shape, dim)


def mask(cond):
    return jnp.where(cond, 1.0, 0.0).astype(BF)


def gate_of(xf, router):
    return jax.nn.sigmoid(jnp.sum(xf * router, -1, keepdims=True))


def inv_of(xf):
    return lax.rsqrt(jnp.mean(xf * xf, -1, keepdims=True) + EPS)


def gelu_and_slope(pre):
    root = 0.7978845608028654
    square = pre * pre
    wave = jnp.tanh(pre * (root + root * 0.044715 * square))
    half = 0.5 + 0.5 * wave
    slope = half + pre * (0.5 - 0.5 * wave * wave) * (root + root * 0.134145 * square)
    return pre * half, slope


def pack_kernel(experts, cap, assign_ref, x_ref, dy_ref, out_ref, slot_ref):
    tok, width = x_ref.shape
    slots = experts * cap
    target = jnp.right_shift(assign_ref[...], tok.bit_length() - 1)
    chosen = mask(iota((experts, tok), 0) == target)
    earlier = mask(iota((tok, tok), 0) < iota((tok, tok), 1))
    ahead = dot(chosen, earlier, ((1,), (0,)))
    rank = jnp.sum(ahead * chosen.astype(F32), 0, keepdims=True)
    slot = target * cap + rank.astype(jnp.int32)
    slot_ref[...] = slot
    place = jnp.where(iota((slots, tok), 0) == slot, 1.0, 0.0)
    empty = FILL - FILL * jnp.sum(place, 1, keepdims=True)
    place = place.astype(BF)
    x = (dot(place, x_ref[...], ((1,), (0,))) + empty).astype(BF)
    out_ref[:, :cap, :] = x.reshape(experts, cap, width)
    dy = dot(place, dy_ref[...], ((1,), (0,))).astype(BF)
    out_ref[:, cap:, :] = dy.reshape(experts, cap, width)


def compact_kernel(buf_ref, x_ref, pos_ref):
    experts, cap, width = buf_ref.shape[0], buf_ref.shape[1] // 2, buf_ref.shape[2]
    slots = experts * cap
    tok = x_ref.shape[0]
    lanes = pos_ref.shape[1]
    rows = buf_ref[:, :cap, :].reshape(slots, width)
    valid = rows[:, :lanes].astype(F32)[:, :1] < 0.5 * FILL
    ones = jnp.broadcast_to(jnp.where(valid, 1.0, 0.0), (slots, lanes))
    bits = cap.bit_length() - 1
    member = mask(jnp.right_shift(iota((experts, slots), 1), bits) == iota((experts, slots), 0))
    counts = dot(member, ones.astype(BF), ((1,), (0,))).astype(BF)
    before = mask(iota((slots, experts), 1) < jnp.right_shift(iota((slots, experts), 0), bits))
    pos = dot(before, counts, ((1,), (0,)))
    pos = pos + jnp.bitwise_and(iota((slots, lanes), 0), cap - 1).astype(F32)
    pos = jnp.where(ones > 0.5, pos, -1.0)
    pos_ref[...] = pos
    pick = mask(iota((tok, slots), 0).astype(F32) == pos.T[:1])
    x_ref[...] = dot(pick, rows, ((1,), (0,))).astype(BF)


def compact_dy_kernel(buf_ref, pos_ref, x_ref, router_ref, dy_ref, db_ref):
    experts, cap, width = buf_ref.shape[0], buf_ref.shape[1] // 2, buf_ref.shape[2]
    tok, slots = x_ref.shape[0], experts * cap
    pick = mask(iota((tok, slots), 0).astype(F32) == pos_ref[...].T[:1])
    dy = dot(pick, buf_ref[:, cap:, :].reshape(slots, width), ((1,), (0,)))
    dy_ref[...] = dy.astype(BF)
    gate = gate_of(x_ref[...].astype(F32), router_ref[...].astype(F32))
    db_ref[...] = (gate * dy).astype(BF)


def forward(x_ref, gain_ref, win_ref, wout_ref, normed_ref, hid_ref):
    xf = x_ref[...].astype(F32)
    normed = (xf * inv_of(xf) * gain_ref[...]).astype(BF)
    normed_ref[...] = normed
    act, slope = gelu_and_slope(dot(normed, win_ref[...], ((1,), (1,))))
    hid = act.astype(BF)
    hid_ref[...] = hid
    return slope, dot(hid, wout_ref[...], ((1,), (0,)))


def backward(x_ref, db_ref, slope, part, gain_ref, router_ref, win_ref, wout_ref, dpre_ref):
    dpre = (slope * dot(db_ref[...], wout_ref[...], ((1,), (1,)))).astype(BF)
    dpre_ref[...] = dpre
    dnormed = dot(dpre, win_ref[...], ((1,), (0,)))
    xf = x_ref[...].astype(F32)
    router = router_ref[...].astype(F32)
    inv = inv_of(xf)
    unit = xf * inv
    dunit = dnormed * gain_ref[...]
    dlogit = (1.0 - gate_of(xf, router)) * jnp.sum(db_ref[...].astype(F32) * part, -1, keepdims=True)
    back = inv * (dunit - unit * jnp.mean(dunit * unit, -1, keepdims=True)) + dlogit * router
    return back, jnp.sum(dnormed * unit, 0, keepdims=True), jnp.sum(dlogit * xf, 0, keepdims=True)


def own_kernel(
    x_ref, db_ref, dy_ref, gain_ref, router_ref, win_ref, wout_ref,
    normed_ref, hid_ref, dpre_ref, part_ref, back_ref, small_ref,
):
    slope, part = forward(x_ref, gain_ref, win_ref, wout_ref, normed_ref, hid_ref)
    part_ref[...] = part
    back, gain_part, router_part = backward(
        x_ref, db_ref, slope, part, gain_ref, router_ref, win_ref, wout_ref, dpre_ref
    )
    back_ref[...] = back + dy_ref[...].astype(F32)
    small_ref[:1, :] = gain_part
    small_ref[1:, :] = router_part


def peer_forward_kernel(x_ref, gain_ref, win_ref, wout_ref, normed_ref, hid_ref, slope_ref, part_ref):
    slope, part = forward(x_ref, gain_ref, win_ref, wout_ref, normed_ref, hid_ref)
    slope_ref[...] = slope.astype(BF)
    part_ref[...] = part.astype(BF)


def peer_backward_kernel(
    x_ref, db_ref, slope_ref, part_ref, small_ref, gain_ref, router_ref, win_ref, wout_ref,
    dpre_ref, back_ref,
):
    tok = x_ref.shape[0]
    back, gain_part, router_part = backward(
        x_ref, db_ref, slope_ref[...].astype(F32), part_ref[...].astype(F32),
        gain_ref, router_ref, win_ref, wout_ref, dpre_ref,
    )
    back_ref[:tok, :] = back.astype(BF)
    small = small_ref[...] + jnp.concatenate([gain_part, router_part], 0)
    high = small.astype(BF)
    rest = small - high.astype(F32)
    middle = rest.astype(BF)
    low = (rest - middle.astype(F32)).astype(BF)
    pad = jnp.zeros((TAIL - 6, small.shape[1]), F32)
    coded = jnp.concatenate([high.astype(F32), middle.astype(F32), low.astype(F32), pad], 0)
    back_ref[tok:, :] = coded.astype(BF)


def grads_kernel(dpo, dpp, no, np_, ho, hp, bo, bp, gin_ref, gout_ref):
    first = ((0,), (0,))
    gin_ref[...] = dot(dpo[...], no[...], first) + dot(dpp[...], np_[...], first)
    gout_ref[...] = dot(ho[...], bo[...], first) + dot(hp[...], bp[...], first)


def spread(pos_ref, rows, out_ref):
    place = mask(iota((out_ref.shape[0], rows.shape[0]), 1).astype(F32) == pos_ref[:, :1])
    out_ref[...] = dot(place, rows, ((1,), (0,))).astype(BF)


def mix_kernel(x_ref, part_ref, recv_ref, router_ref, pos_ref, out_ref):
    xf = x_ref[...].astype(F32)
    gate = gate_of(xf, router_ref[...].astype(F32))
    rows = (xf + gate * (part_ref[...] + recv_ref[...].astype(F32))).astype(BF)
    spread(pos_ref, rows, out_ref)


def decode(ref, tok):
    coded = ref[tok:, :].astype(F32)
    return coded[0:2] + coded[2:4] + coded[4:6]


def add_kernel(own_ref, sent_ref, recv_ref, pos_ref, out_ref, small_ref):
    tok = own_ref.shape[0]
    rows = (own_ref[...] + recv_ref[:tok, :].astype(F32)).astype(BF)
    spread(pos_ref, rows, out_ref)
    small_ref[...] = decode(sent_ref, tok) + decode(recv_ref, tok)


def unpack_kernel(slot_ref, buf_ref, out_ref):
    slots, tok = buf_ref.shape[0], out_ref.shape[0]
    place = mask(iota((slots, tok), 0) == slot_ref[...])
    out_ref[...] = dot(place, buf_ref[...], ((0,), (0,))).astype(BF)


def call(kernel, name, out_shape, flops, moved, inputs, after=None, vmem=32, **kw):
    if after is not None:
        count = len(inputs)
        inner = kernel

        def kernel(*refs):
            inner(*refs[:count], *refs[count + 1:])

        specs = kw.get("in_specs", [pl.BlockSpec(memory_space=pltpu.VMEM)] * count)
        kw["in_specs"] = [*specs, pl.BlockSpec(memory_space=pl.ANY)]
        inputs = (*inputs, after)
    return pl.pallas_call(
        kernel,
        name=name,
        out_shape=out_shape,
        compiler_params=pltpu.CompilerParams(vmem_limit_bytes=vmem * MIB),
        cost_estimate=pl.CostEstimate(flops=flops, bytes_accessed=moved, transcendentals=0),
        **kw,
    )(*inputs)


def shape(dims, dtype):
    return jax.ShapeDtypeStruct(dims, dtype)


def swap(values):
    return lax.ppermute(values, "dp", SWAP)


def exchange(buffer, experts):
    return lax.all_to_all(buffer, "expert", split_axis=0, concat_axis=0, tiled=True)


def local(tokens, cotangent, assign, gain, router, w_in, w_out):
    experts = lax.axis_size("expert")
    tok, width = tokens.shape[1:]
    cap = 2 * tok // experts
    slots = experts * cap
    win, wout = w_in[0], w_out[0]
    hidden = win.shape[0]
    place_cost = 2 * slots * tok * width
    mm = 2 * tok * width * hidden
    rows_bf = shape((tok, width), BF)
    hid_bf = shape((tok, hidden), BF)
    slots_bf = shape((slots, width), BF)

    packed, slot = call(
        functools.partial(pack_kernel, experts, cap), "pack",
        (shape((experts, 2 * cap, width), BF), shape((1, tok), jnp.int32)),
        2 * place_cost, 6 * MIB, (assign, tokens[0], cotangent[0]),
    )
    buf = exchange(packed, experts)
    x_own, pos = call(
        compact_kernel, "compact_x", (rows_bf, shape((slots, 128), F32)), place_cost, 3 * MIB, (buf,)
    )
    x_peer = swap(x_own)
    dy_own, db_own = call(
        compact_dy_kernel, "compact_dy", (rows_bf, rows_bf), place_cost, 4 * MIB, (buf, pos, x_own, router)
    )
    db_peer = swap(db_own)
    normed_o, hid_o, dpre_o, part_o, back_o, small_o = call(
        own_kernel, "own",
        (rows_bf, hid_bf, hid_bf, shape((tok, width), F32), shape((tok, width), F32), shape((2, width), F32)),
        4 * mm, 14 * MIB, (x_own, db_own, dy_own, gain, router, win, wout),
    )
    normed_p, hid_p, slope_p, part_p = call(
        peer_forward_kernel, "peer_forward", (rows_bf, hid_bf, hid_bf, rows_bf),
        2 * mm, 9 * MIB, (x_peer, gain, win, wout), small_o,
    )
    part_recv = swap(part_p)
    dpre_p, back_p = call(
        peer_backward_kernel, "peer_backward", (hid_bf, shape((tok + TAIL, width), BF)),
        2 * mm, 9 * MIB, (x_peer, db_peer, slope_p, part_p, small_o, gain, router, win, wout),
    )
    back_recv = swap(back_p)
    y_pack = call(
        mix_kernel, "mix", slots_bf, place_cost, 8 * MIB, (x_own, part_o, part_recv, router, pos)
    )
    half = hidden // 2
    left = pl.BlockSpec((tok, half), lambda i: (0, i))
    right = pl.BlockSpec((tok, width), lambda i: (0, 0))
    grad = pl.BlockSpec((half, width), lambda i: (i, 0))
    gin, gout = call(
        grads_kernel, "weight_grads", (shape((hidden, width), F32), shape((hidden, width), F32)),
        GF, 16 * MIB, (dpre_o, dpre_p, normed_o, normed_p, hid_o, hid_p, db_own, db_peer), y_pack,
        grid=(2,),
        in_specs=[left, left, right, right, left, left, right, right],
        out_specs=(grad, grad),
    )
    y_buf = exchange(y_pack.reshape(experts, cap, width), experts).reshape(slots, width)
    back_pack, small = call(
        add_kernel, "add_back", (slots_bf, shape((2, width), F32)), place_cost, 5 * MIB,
        (back_o, back_p, back_recv, pos), gin,
    )
    back_pack, y_buf = lax.optimization_barrier((back_pack, y_buf))
    back_buf = exchange(back_pack.reshape(experts, cap, width), experts).reshape(slots, width)
    mixed = call(unpack_kernel, "unpack", rows_bf, place_cost, 3 * MIB, (slot, y_buf))
    input_grad = call(unpack_kernel, "unpack", rows_bf, place_cost, 3 * MIB, (slot, back_buf), mixed)
    return (mixed[None], input_grad[None], gin[None], gout[None], small[:1], small[1:])


def solution(mesh):
    return jax.shard_map(
        local,
        mesh=mesh,
        in_specs=(
            P("dp", "expert", None),
            P("dp", "expert", None),
            P("dp", "expert"),
            P("expert", None),
            P("expert", None),
            P("expert", "dp", None),
            P("expert", "dp", None),
        ),
        out_specs=(
            P("dp", "expert", None),
            P("dp", "expert", None),
            P("expert", "dp", None),
            P("expert", "dp", None),
            P("expert", None),
            P("expert", None),
        ),
        check_vma=False,
    )
```

```python
import functools

import jax
import jax.numpy as jnp
from jax import lax
from jax.experimental import pallas as pl
from jax.experimental.pallas import tpu as pltpu
from jax.sharding import PartitionSpec as P

EPS = 1e-05
FILL = 64.0
SWAP = ((0, 1), (1, 0))
BF = jnp.bfloat16
F32 = jnp.float32
MIB = 1024 * 1024
TAIL = 16
LONG = 10**12


def dot(left, right, dims):
    return lax.dot_general(left, right, (dims, ((), ())), preferred_element_type=F32)


def iota(shape, dim):
    return lax.broadcasted_iota(jnp.int32, shape, dim)


def mask(cond):
    return jnp.where(cond, 1.0, 0.0).astype(BF)


def gate_of(xf, router):
    return jax.nn.sigmoid(jnp.sum(xf * router, -1, keepdims=True))


def inv_of(xf):
    return lax.rsqrt(jnp.mean(xf * xf, -1, keepdims=True) + EPS)


def gelu_and_slope(pre):
    root = 0.7978845608028654
    square = pre * pre
    wave = jnp.tanh(pre * (root + root * 0.044715 * square))
    half = 0.5 + 0.5 * wave
    slope = half + pre * (0.5 - 0.5 * wave * wave) * (root + root * 0.134145 * square)
    return pre * half, slope


def copies(pairs, sems, first=0):
    return [pltpu.make_async_copy(src, dst, sems.at[first + i]) for i, (src, dst) in enumerate(pairs)]


def pieces(src, dst, count):
    step = src.shape[0] // count
    return [(src.at[pl.ds(i * step, step)], dst.at[pl.ds(i * step, step)]) for i in range(count)]


def start(group):
    for copy in group:
        copy.start()


def wait(group):
    for copy in group:
        copy.wait()


def pack_kernel(experts, cap, assign_ref, x_ref, dy_ref, out_ref, slot_ref):
    tok, width = x_ref.shape
    slots = experts * cap
    target = jnp.right_shift(assign_ref[...], tok.bit_length() - 1)
    chosen = mask(iota((experts, tok), 0) == target)
    earlier = mask(iota((tok, tok), 0) < iota((tok, tok), 1))
    ahead = dot(chosen, earlier, ((1,), (0,)))
    rank = jnp.sum(ahead * chosen.astype(F32), 0, keepdims=True)
    slot = target * cap + rank.astype(jnp.int32)
    slot_ref[...] = slot
    place = jnp.where(iota((slots, tok), 0) == slot, 1.0, 0.0)
    empty = FILL - FILL * jnp.sum(place, 1, keepdims=True)
    place = place.astype(BF)
    x = (dot(place, x_ref[...], ((1,), (0,))) + empty).astype(BF)
    out_ref[:, :cap, :] = x.reshape(experts, cap, width)
    dy = dot(place, dy_ref[...], ((1,), (0,))).astype(BF)
    out_ref[:, cap:, :] = dy.reshape(experts, cap, width)


def compact_kernel(buf_ref, x_ref, pos_ref):
    experts, cap, width = buf_ref.shape[0], buf_ref.shape[1] // 2, buf_ref.shape[2]
    slots = experts * cap
    tok = x_ref.shape[0]
    lanes = pos_ref.shape[1]
    rows = buf_ref[:, :cap, :].reshape(slots, width)
    valid = rows[:, :lanes].astype(F32)[:, :1] < 0.5 * FILL
    ones = jnp.broadcast_to(jnp.where(valid, 1.0, 0.0), (slots, lanes))
    bits = cap.bit_length() - 1
    member = mask(jnp.right_shift(iota((experts, slots), 1), bits) == iota((experts, slots), 0))
    counts = dot(member, ones.astype(BF), ((1,), (0,))).astype(BF)
    before = mask(iota((slots, experts), 1) < jnp.right_shift(iota((slots, experts), 0), bits))
    pos = dot(before, counts, ((1,), (0,)))
    pos = pos + jnp.bitwise_and(iota((slots, lanes), 0), cap - 1).astype(F32)
    pos = jnp.where(ones > 0.5, pos, -1.0)
    pos_ref[...] = pos
    pick = mask(iota((tok, slots), 0).astype(F32) == pos.T[:1])
    x_ref[...] = dot(pick, rows, ((1,), (0,))).astype(BF)


def compact_dy_kernel(buf_ref, pos_ref, x_ref, router_ref, dy_ref, db_ref):
    experts, cap, width = buf_ref.shape[0], buf_ref.shape[1] // 2, buf_ref.shape[2]
    tok, slots = x_ref.shape[0], experts * cap
    pick = mask(iota((tok, slots), 0).astype(F32) == pos_ref[...].T[:1])
    dy = dot(pick, buf_ref[:, cap:, :].reshape(slots, width), ((1,), (0,)))
    dy_ref[...] = dy.astype(BF)
    gate = gate_of(x_ref[...].astype(F32), router_ref[...].astype(F32))
    db_ref[...] = (gate * dy).astype(BF)


def forward(x_ref, gain_ref, win_ref, wout_ref, normed_ref, hid_ref):
    xf = x_ref[...].astype(F32)
    normed = (xf * inv_of(xf) * gain_ref[...]).astype(BF)
    normed_ref[...] = normed
    act, slope = gelu_and_slope(dot(normed, win_ref[...], ((1,), (1,))))
    hid = act.astype(BF)
    hid_ref[...] = hid
    return slope, dot(hid, wout_ref[...], ((1,), (0,)))


def backward(x_ref, db_ref, slope, part, gain_ref, router_ref, win_ref, wout_ref, dpre_ref):
    dpre = (slope * dot(db_ref[...], wout_ref[...], ((1,), (1,)))).astype(BF)
    dpre_ref[...] = dpre
    dnormed = dot(dpre, win_ref[...], ((1,), (0,)))
    xf = x_ref[...].astype(F32)
    router = router_ref[...].astype(F32)
    inv = inv_of(xf)
    unit = xf * inv
    dunit = dnormed * gain_ref[...]
    dlogit = (1.0 - gate_of(xf, router)) * jnp.sum(db_ref[...].astype(F32) * part, -1, keepdims=True)
    back = inv * (dunit - unit * jnp.mean(dunit * unit, -1, keepdims=True)) + dlogit * router
    return back, jnp.sum(dnormed * unit, 0, keepdims=True), jnp.sum(dlogit * xf, 0, keepdims=True)


def own_kernel(
    x_ref, db_ref, dy_ref, gain_ref, router_ref, win_ref, wout_ref,
    normed_ref, hid_ref, dpre_ref, part_ref, back_ref, small_ref,
):
    slope, part = forward(x_ref, gain_ref, win_ref, wout_ref, normed_ref, hid_ref)
    part_ref[...] = part
    back, gain_part, router_part = backward(
        x_ref, db_ref, slope, part, gain_ref, router_ref, win_ref, wout_ref, dpre_ref
    )
    back_ref[...] = back + dy_ref[...].astype(F32)
    small_ref[:1, :] = gain_part
    small_ref[1:, :] = router_part


def peer_forward_kernel(x_ref, gain_ref, win_ref, wout_ref, normed_ref, hid_ref, slope_ref, part_ref):
    slope, part = forward(x_ref, gain_ref, win_ref, wout_ref, normed_ref, hid_ref)
    slope_ref[...] = slope.astype(BF)
    part_ref[...] = part.astype(BF)


def peer_backward_kernel(
    x_ref, db_ref, slope_ref, part_ref, small_ref, gain_ref, router_ref, win_ref, wout_ref,
    dpre_ref, back_ref, tail_ref,
):
    tok = x_ref.shape[0]
    back, gain_part, router_part = backward(
        x_ref, db_ref, slope_ref[...].astype(F32), part_ref[...].astype(F32),
        gain_ref, router_ref, win_ref, wout_ref, dpre_ref,
    )
    back_ref[:tok, :] = back.astype(BF)
    small = small_ref[...] + jnp.concatenate([gain_part, router_part], 0)
    high = small.astype(BF)
    rest = small - high.astype(F32)
    middle = rest.astype(BF)
    low = (rest - middle.astype(F32)).astype(BF)
    pad = jnp.zeros((TAIL - 6, small.shape[1]), F32)
    coded = jnp.concatenate([high.astype(F32), middle.astype(F32), low.astype(F32), pad], 0)
    back_ref[tok:, :] = coded.astype(BF)
    tail_ref[...] = coded.astype(BF)


def grads_kernel(dpo, dpp, no, np_, ho, hp, bo, bp, gin_ref, gout_ref, done_ref):
    done_ref[...] = jnp.zeros_like(done_ref)
    first = ((0,), (0,))
    gin_ref[...] = dot(dpo[...], no[...], first) + dot(dpp[...], np_[...], first)
    gout_ref[...] = dot(ho[...], bo[...], first) + dot(hp[...], bp[...], first)


def spread(pos_ref, rows, out_ref):
    place = mask(iota((out_ref.shape[0], rows.shape[0]), 1).astype(F32) == pos_ref[:, :1])
    out_ref[...] = dot(place, rows, ((1,), (0,))).astype(BF)


def mix_kernel(x_ref, part_ref, recv_ref, router_ref, pos_ref, out_ref, done_ref):
    done_ref[...] = jnp.zeros_like(done_ref)
    xf = x_ref[...].astype(F32)
    gate = gate_of(xf, router_ref[...].astype(F32))
    rows = (xf + gate * (part_ref[...] + recv_ref[...].astype(F32))).astype(BF)
    spread(pos_ref, rows, out_ref)


def decode(ref, tok):
    coded = ref[tok : tok + TAIL, :].astype(F32)
    return coded[0:2] + coded[2:4] + coded[4:6]


def add_kernel(own_ref, tail_ref, recv_ref, pos_ref, out_ref, small_ref, recv, out, sems):
    tok, slots = own_ref.shape[0], out.shape[0]
    loads = copies(pieces(recv_ref, recv, 3), sems)
    start(loads)
    place = mask(iota((slots, tok), 1).astype(F32) == pos_ref[:, :1])
    wait(loads)
    rows = (own_ref[...] + recv[:tok, :].astype(F32)).astype(BF)
    step = slots // 2
    stores = []
    for part in range(2):
        at = pl.ds(part * step, step)
        out[at, :] = dot(place[part * step : (part + 1) * step], rows, ((1,), (0,))).astype(BF)
        group = copies(pieces(out.at[at], out_ref.at[at], 2), sems, 3 + 2 * part)
        start(group)
        stores += group
    small_ref[...] = decode(tail_ref, 0) + decode(recv, tok)
    wait(stores)


def unpack_kernel(slot_ref, buf_ref, out_ref, place_ref):
    slots, tok = buf_ref.shape[0], out_ref.shape[0]
    place = mask(iota((tok, slots), 1) == jnp.broadcast_to(slot_ref[...], (128, tok)).T[:, :1])
    place_ref[...] = place
    out_ref[...] = dot(place, buf_ref[...], ((1,), (0,))).astype(BF)


def unpack_last_kernel(place_ref, buf_ref, out_ref, buf, out, sems):
    loads = copies(pieces(buf_ref, buf, 4), sems)
    start(loads)
    wait(loads)
    step = out.shape[0] // 2
    stores = []
    for part in range(2):
        at = pl.ds(part * step, step)
        out[at, :] = dot(place_ref[at, :], buf[...], ((1,), (0,))).astype(BF)
        group = copies(pieces(out.at[at], out_ref.at[at], 2), sems, 4 + 2 * part)
        start(group)
        stores += group
    wait(stores)


def call(kernel, name, out_shape, flops, moved, inputs, after=None, vmem=32, **kw):
    if after is not None:
        count = len(inputs)
        inner = kernel

        def kernel(*refs):
            inner(*refs[:count], *refs[count + 1:])

        specs = kw.get("in_specs", [pl.BlockSpec(memory_space=pltpu.VMEM)] * count)
        kw["in_specs"] = [*specs, pl.BlockSpec(memory_space=pl.ANY)]
        inputs = (*inputs, after)
    return pl.pallas_call(
        kernel,
        name=name,
        out_shape=out_shape,
        compiler_params=pltpu.CompilerParams(vmem_limit_bytes=vmem * MIB),
        cost_estimate=pl.CostEstimate(flops=flops, bytes_accessed=moved, transcendentals=0),
        **kw,
    )(*inputs)


def shape(dims, dtype):
    return jax.ShapeDtypeStruct(dims, dtype)


def swap(values):
    return lax.ppermute(values, "dp", SWAP)


def exchange(buffer, experts):
    return lax.all_to_all(buffer, "expert", split_axis=0, concat_axis=0, tiled=True)


def local(tokens, cotangent, assign, gain, router, w_in, w_out):
    experts = lax.axis_size("expert")
    tok, width = tokens.shape[1:]
    cap = 2 * tok // experts
    slots = experts * cap
    win, wout = w_in[0], w_out[0]
    hidden = win.shape[0]
    place_cost = 2 * slots * tok * width
    mm = 2 * tok * width * hidden
    rows_bf = shape((tok, width), BF)
    hid_bf = shape((tok, hidden), BF)
    slots_bf = shape((slots, width), BF)

    outer = pl.BlockSpec(memory_space=pltpu.HBM)
    inside = pl.BlockSpec(memory_space=pltpu.VMEM)
    packed, slot = call(
        functools.partial(pack_kernel, experts, cap), "pack",
        (shape((experts, 2 * cap, width), BF), shape((1, tok), jnp.int32)),
        2 * place_cost, 6 * MIB, (assign, tokens[0], cotangent[0]),
    )
    buf = exchange(packed, experts)
    x_own, pos = call(
        compact_kernel, "compact_x", (rows_bf, shape((slots, 128), F32)), place_cost, 3 * MIB, (buf,)
    )
    x_peer = swap(x_own)
    dy_own, db_own = call(
        compact_dy_kernel, "compact_dy", (rows_bf, rows_bf), place_cost, 4 * MIB, (buf, pos, x_own, router)
    )
    db_peer = swap(db_own)
    normed_o, hid_o, dpre_o, part_o, back_o, small_o = call(
        own_kernel, "own",
        (rows_bf, hid_bf, hid_bf, shape((tok, width), F32), shape((tok, width), F32), shape((2, width), F32)),
        4 * mm, 14 * MIB, (x_own, db_own, dy_own, gain, router, win, wout),
    )
    normed_p, hid_p, slope_p, part_p = call(
        peer_forward_kernel, "peer_forward", (rows_bf, hid_bf, hid_bf, rows_bf),
        2 * mm, 9 * MIB, (x_peer, gain, win, wout), small_o,
    )
    part_recv = swap(part_p)
    dpre_p, back_p, tail = call(
        peer_backward_kernel, "peer_backward", (hid_bf, shape((tok + TAIL, width), BF), shape((TAIL, width), BF)),
        2 * mm, 9 * MIB, (x_peer, db_peer, slope_p, part_p, small_o, gain, router, win, wout),
    )
    back_recv = swap(back_p)
    y_pack, mix_done = call(
        mix_kernel, "mix", (slots_bf, shape((8, 128), F32)), place_cost, 8 * MIB, (x_own, part_o, part_recv, router, pos)
    )
    half = hidden // 2
    left = pl.BlockSpec((tok, half), lambda i: (0, i))
    right = pl.BlockSpec((tok, width), lambda i: (0, 0))
    grad = pl.BlockSpec((half, width), lambda i: (i, 0))
    token = shape((8, 128), F32)
    gin, gout, grads_done = call(
        grads_kernel, "weight_grads", (shape((hidden, width), F32), shape((hidden, width), F32), token),
        LONG, 16 * MIB, (dpre_o, dpre_p, normed_o, normed_p, hid_o, hid_p, db_own, db_peer), mix_done,
        grid=(2,),
        in_specs=[left, left, right, right, left, left, right, right],
        out_specs=(grad, grad, pl.BlockSpec((8, 128), lambda i: (0, 0))),
    )
    y_buf = exchange(y_pack.reshape(experts, cap, width), experts).reshape(slots, width)
    back_pack, small = call(
        add_kernel, "add_back", (slots_bf, shape((2, width), F32)), place_cost, 5 * MIB,
        (back_o, tail, back_recv, pos), grads_done, 24,
        in_specs=[inside, inside, outer, inside],
        out_specs=(outer, inside),
        scratch_shapes=[
            pltpu.VMEM((tok + TAIL, width), BF),
            pltpu.VMEM((slots, width), BF),
            pltpu.SemaphoreType.DMA((7,)),
        ],
    )
    back_pack, y_buf = lax.optimization_barrier((back_pack, y_buf))
    back_buf = exchange(back_pack.reshape(experts, cap, width), experts).reshape(slots, width)
    mixed, place = call(
        unpack_kernel, "unpack", (rows_bf, shape((tok, slots), BF)), place_cost, 4 * MIB, (slot, y_buf)
    )
    input_grad = call(
        unpack_last_kernel, "unpack_last", rows_bf, place_cost, 4 * MIB, (place, back_buf), None, 40,
        in_specs=[inside, outer],
        out_specs=outer,
        scratch_shapes=[
            pltpu.VMEM((slots, width), BF),
            pltpu.VMEM((tok, width), BF),
            pltpu.SemaphoreType.DMA((8,)),
        ],
    )
    return (mixed[None], input_grad[None], gin[None], gout[None], small[:1], small[1:])


def solution(mesh):
    return jax.shard_map(
        local,
        mesh=mesh,
        in_specs=(
            P("dp", "expert", None),
            P("dp", "expert", None),
            P("dp", "expert"),
            P("expert", None),
            P("expert", None),
            P("expert", "dp", None),
            P("expert", "dp", None),
        ),
        out_specs=(
            P("dp", "expert", None),
            P("dp", "expert", None),
            P("expert", "dp", None),
            P("expert", "dp", None),
            P("expert", None),
            P("expert", None),
        ),
        check_vma=False,
    )
```

```python
import functools

import jax
import jax.numpy as jnp
from jax import lax
from jax.experimental import pallas as pl
from jax.experimental.pallas import tpu as pltpu
from jax.sharding import PartitionSpec as P

EPS = 1e-05
FILL = 64.0
SWAP = ((0, 1), (1, 0))
BF = jnp.bfloat16
F32 = jnp.float32
MIB = 1024 * 1024
TAIL = 16
LONG = 10**12


def dot(left, right, dims):
    return lax.dot_general(left, right, (dims, ((), ())), preferred_element_type=F32)


def iota(shape, dim):
    return lax.broadcasted_iota(jnp.int32, shape, dim)


def mask(cond):
    return jnp.where(cond, 1.0, 0.0).astype(BF)


def gate_of(xf, router):
    return jax.nn.sigmoid(jnp.sum(xf * router, -1, keepdims=True))


def inv_of(xf):
    return lax.rsqrt(jnp.mean(xf * xf, -1, keepdims=True) + EPS)


def gelu_and_slope(pre):
    root = 0.7978845608028654
    square = pre * pre
    wave = jnp.tanh(pre * (root + root * 0.044715 * square))
    half = 0.5 + 0.5 * wave
    slope = half + pre * (0.5 - 0.5 * wave * wave) * (root + root * 0.134145 * square)
    return pre * half, slope


def copies(pairs, sems, first=0):
    return [pltpu.make_async_copy(src, dst, sems.at[first + i]) for i, (src, dst) in enumerate(pairs)]


def pieces(src, dst, count):
    step = src.shape[0] // count
    return [(src.at[pl.ds(i * step, step)], dst.at[pl.ds(i * step, step)]) for i in range(count)]


def start(group):
    for copy in group:
        copy.start()


def wait(group):
    for copy in group:
        copy.wait()


def pack_kernel(experts, cap, assign_ref, x_ref, dy_ref, out_ref, slot_ref):
    tok, width = x_ref.shape
    slots = experts * cap
    target = jnp.right_shift(assign_ref[...], tok.bit_length() - 1)
    chosen = mask(iota((experts, tok), 0) == target)
    earlier = mask(iota((tok, tok), 0) < iota((tok, tok), 1))
    ahead = dot(chosen, earlier, ((1,), (0,)))
    rank = jnp.sum(ahead * chosen.astype(F32), 0, keepdims=True)
    slot = target * cap + rank.astype(jnp.int32)
    slot_ref[...] = slot
    place = jnp.where(iota((slots, tok), 0) == slot, 1.0, 0.0)
    empty = FILL - FILL * jnp.sum(place, 1, keepdims=True)
    place = place.astype(BF)
    x = (dot(place, x_ref[...], ((1,), (0,))) + empty).astype(BF)
    out_ref[:, :cap, :] = x.reshape(experts, cap, width)
    dy = dot(place, dy_ref[...], ((1,), (0,))).astype(BF)
    out_ref[:, cap:, :] = dy.reshape(experts, cap, width)


def compact_kernel(buf_ref, x_ref, pos_ref):
    experts, cap, width = buf_ref.shape[0], buf_ref.shape[1] // 2, buf_ref.shape[2]
    slots = experts * cap
    tok = x_ref.shape[0]
    lanes = pos_ref.shape[1]
    rows = buf_ref[:, :cap, :].reshape(slots, width)
    valid = rows[:, :lanes].astype(F32)[:, :1] < 0.5 * FILL
    ones = jnp.broadcast_to(jnp.where(valid, 1.0, 0.0), (slots, lanes))
    bits = cap.bit_length() - 1
    member = mask(jnp.right_shift(iota((experts, slots), 1), bits) == iota((experts, slots), 0))
    counts = dot(member, ones.astype(BF), ((1,), (0,))).astype(BF)
    before = mask(iota((slots, experts), 1) < jnp.right_shift(iota((slots, experts), 0), bits))
    pos = dot(before, counts, ((1,), (0,)))
    pos = pos + jnp.bitwise_and(iota((slots, lanes), 0), cap - 1).astype(F32)
    pos = jnp.where(ones > 0.5, pos, -1.0)
    pos_ref[...] = pos
    pick = mask(iota((tok, slots), 0).astype(F32) == pos.T[:1])
    x_ref[...] = dot(pick, rows, ((1,), (0,))).astype(BF)


def compact_dy_kernel(buf_ref, pos_ref, x_ref, router_ref, dy_ref, db_ref):
    experts, cap, width = buf_ref.shape[0], buf_ref.shape[1] // 2, buf_ref.shape[2]
    tok, slots = x_ref.shape[0], experts * cap
    pick = mask(iota((tok, slots), 0).astype(F32) == pos_ref[...].T[:1])
    dy = dot(pick, buf_ref[:, cap:, :].reshape(slots, width), ((1,), (0,)))
    dy_ref[...] = dy.astype(BF)
    gate = gate_of(x_ref[...].astype(F32), router_ref[...].astype(F32))
    db_ref[...] = (gate * dy).astype(BF)


def forward(x_ref, gain_ref, win_ref, wout_ref, normed_ref, hid_ref):
    xf = x_ref[...].astype(F32)
    normed = (xf * inv_of(xf) * gain_ref[...]).astype(BF)
    normed_ref[...] = normed
    act, slope = gelu_and_slope(dot(normed, win_ref[...], ((1,), (1,))))
    hid = act.astype(BF)
    hid_ref[...] = hid
    return slope, dot(hid, wout_ref[...], ((1,), (0,)))


def backward(x_ref, db_ref, slope, part, gain_ref, router_ref, win_ref, wout_ref, dpre_ref):
    dpre = (slope * dot(db_ref[...], wout_ref[...], ((1,), (1,)))).astype(BF)
    dpre_ref[...] = dpre
    dnormed = dot(dpre, win_ref[...], ((1,), (0,)))
    xf = x_ref[...].astype(F32)
    router = router_ref[...].astype(F32)
    inv = inv_of(xf)
    unit = xf * inv
    dunit = dnormed * gain_ref[...]
    dlogit = (1.0 - gate_of(xf, router)) * jnp.sum(db_ref[...].astype(F32) * part, -1, keepdims=True)
    back = inv * (dunit - unit * jnp.mean(dunit * unit, -1, keepdims=True)) + dlogit * router
    return back, jnp.sum(dnormed * unit, 0, keepdims=True), jnp.sum(dlogit * xf, 0, keepdims=True)


def own_kernel(
    x_ref, db_ref, dy_ref, pos_ref, gain_ref, router_ref, win_ref, wout_ref,
    normed_ref, hid_ref, dpre_ref, base_ref, back_ref, small_ref, place_ref, gate_ref,
):
    slope, part = forward(x_ref, gain_ref, win_ref, wout_ref, normed_ref, hid_ref)
    xf = x_ref[...].astype(F32)
    gate = gate_of(xf, router_ref[...].astype(F32))
    base_ref[...] = xf + gate * part
    gate_ref[...] = jnp.broadcast_to(gate, gate_ref.shape)
    place_ref[...] = mask(iota(place_ref.shape, 1).astype(F32) == pos_ref[:, :1])
    back, gain_part, router_part = backward(
        x_ref, db_ref, slope, part, gain_ref, router_ref, win_ref, wout_ref, dpre_ref
    )
    back_ref[...] = back + dy_ref[...].astype(F32)
    small_ref[:1, :] = gain_part
    small_ref[1:, :] = router_part


def peer_forward_kernel(x_ref, gain_ref, win_ref, wout_ref, normed_ref, hid_ref, slope_ref, part_ref):
    slope, part = forward(x_ref, gain_ref, win_ref, wout_ref, normed_ref, hid_ref)
    slope_ref[...] = slope.astype(BF)
    part_ref[...] = part.astype(BF)


def peer_backward_kernel(
    x_ref, db_ref, slope_ref, part_ref, small_ref, gain_ref, router_ref, win_ref, wout_ref,
    dpre_ref, back_ref, tail_ref,
):
    tok = x_ref.shape[0]
    back, gain_part, router_part = backward(
        x_ref, db_ref, slope_ref[...].astype(F32), part_ref[...].astype(F32),
        gain_ref, router_ref, win_ref, wout_ref, dpre_ref,
    )
    back_ref[:tok, :] = back.astype(BF)
    small = small_ref[...] + jnp.concatenate([gain_part, router_part], 0)
    high = small.astype(BF)
    rest = small - high.astype(F32)
    middle = rest.astype(BF)
    low = (rest - middle.astype(F32)).astype(BF)
    pad = jnp.zeros((TAIL - 6, small.shape[1]), F32)
    coded = jnp.concatenate([high.astype(F32), middle.astype(F32), low.astype(F32), pad], 0)
    back_ref[tok:, :] = coded.astype(BF)
    tail_ref[...] = coded.astype(BF)


def grads_kernel(dpo, dpp, no, np_, ho, hp, bo, bp, gin_ref, gout_ref, done_ref):
    done_ref[...] = jnp.zeros_like(done_ref)
    first = ((0,), (0,))
    gin_ref[...] = dot(dpo[...], no[...], first) + dot(dpp[...], np_[...], first)
    gout_ref[...] = dot(ho[...], bo[...], first) + dot(hp[...], bp[...], first)


def mix_kernel(base_ref, gate_ref, recv_ref, place_ref, out_ref, done_ref):
    done_ref[...] = jnp.zeros_like(done_ref)
    rows = (base_ref[...] + gate_ref[:, :1] * recv_ref[...].astype(F32)).astype(BF)
    out_ref[...] = dot(place_ref[...], rows, ((1,), (0,))).astype(BF)


def decode(ref, tok):
    coded = ref[tok : tok + TAIL, :].astype(F32)
    return coded[0:2] + coded[2:4] + coded[4:6]


def add_kernel(own_ref, tail_ref, recv_ref, place_ref, out_ref, small_ref, recv, out, sems):
    tok, slots = own_ref.shape[0], out.shape[0]
    loads = copies(pieces(recv_ref, recv, 3), sems)
    start(loads)
    wait(loads)
    rows = (own_ref[...] + recv[:tok, :].astype(F32)).astype(BF)
    step = slots // 2
    stores = []
    for part in range(2):
        at = pl.ds(part * step, step)
        out[at, :] = dot(place_ref[at, :], rows, ((1,), (0,))).astype(BF)
        group = copies(pieces(out.at[at], out_ref.at[at], 2), sems, 3 + 2 * part)
        start(group)
        stores += group
    small_ref[...] = decode(tail_ref, 0) + decode(recv, tok)
    wait(stores)


def unpack_kernel(slot_ref, buf_ref, out_ref, place_ref):
    slots, tok = buf_ref.shape[0], out_ref.shape[0]
    place = mask(iota((tok, slots), 1) == jnp.broadcast_to(slot_ref[...], (128, tok)).T[:, :1])
    place_ref[...] = place
    out_ref[...] = dot(place, buf_ref[...], ((1,), (0,))).astype(BF)


def unpack_last_kernel(place_ref, buf_ref, out_ref, buf, out, sems):
    loads = copies(pieces(buf_ref, buf, 4), sems)
    start(loads)
    wait(loads)
    step = out.shape[0] // 2
    stores = []
    for part in range(2):
        at = pl.ds(part * step, step)
        out[at, :] = dot(place_ref[at, :], buf[...], ((1,), (0,))).astype(BF)
        group = copies(pieces(out.at[at], out_ref.at[at], 2), sems, 4 + 2 * part)
        start(group)
        stores += group
    wait(stores)


def call(kernel, name, out_shape, flops, moved, inputs, after=None, vmem=32, **kw):
    if after is not None:
        count = len(inputs)
        inner = kernel

        def kernel(*refs):
            inner(*refs[:count], *refs[count + 1:])

        specs = kw.get("in_specs", [pl.BlockSpec(memory_space=pltpu.VMEM)] * count)
        kw["in_specs"] = [*specs, pl.BlockSpec(memory_space=pl.ANY)]
        inputs = (*inputs, after)
    return pl.pallas_call(
        kernel,
        name=name,
        out_shape=out_shape,
        compiler_params=pltpu.CompilerParams(vmem_limit_bytes=vmem * MIB),
        cost_estimate=pl.CostEstimate(flops=flops, bytes_accessed=moved, transcendentals=0),
        **kw,
    )(*inputs)


def shape(dims, dtype):
    return jax.ShapeDtypeStruct(dims, dtype)


def swap(values):
    return lax.ppermute(values, "dp", SWAP)


def exchange(buffer, experts):
    return lax.all_to_all(buffer, "expert", split_axis=0, concat_axis=0, tiled=True)


def local(tokens, cotangent, assign, gain, router, w_in, w_out):
    experts = lax.axis_size("expert")
    tok, width = tokens.shape[1:]
    cap = 2 * tok // experts
    slots = experts * cap
    win, wout = w_in[0], w_out[0]
    hidden = win.shape[0]
    place_cost = 2 * slots * tok * width
    mm = 2 * tok * width * hidden
    rows_bf = shape((tok, width), BF)
    hid_bf = shape((tok, hidden), BF)
    slots_bf = shape((slots, width), BF)

    outer = pl.BlockSpec(memory_space=pltpu.HBM)
    inside = pl.BlockSpec(memory_space=pltpu.VMEM)
    packed, slot = call(
        functools.partial(pack_kernel, experts, cap), "pack",
        (shape((experts, 2 * cap, width), BF), shape((1, tok), jnp.int32)),
        2 * place_cost, 6 * MIB, (assign, tokens[0], cotangent[0]),
    )
    buf = exchange(packed, experts)
    x_own, pos = call(
        compact_kernel, "compact_x", (rows_bf, shape((slots, 128), F32)), place_cost, 3 * MIB, (buf,)
    )
    x_peer = swap(x_own)
    dy_own, db_own = call(
        compact_dy_kernel, "compact_dy", (rows_bf, rows_bf), place_cost, 4 * MIB, (buf, pos, x_own, router)
    )
    db_peer = swap(db_own)
    normed_o, hid_o, dpre_o, base_o, back_o, small_o, place, gate = call(
        own_kernel, "own",
        (rows_bf, hid_bf, hid_bf, shape((tok, width), F32), shape((tok, width), F32), shape((2, width), F32),
         shape((slots, tok), BF), shape((tok, 128), F32)),
        4 * mm, 14 * MIB, (x_own, db_own, dy_own, pos, gain, router, win, wout),
    )
    normed_p, hid_p, slope_p, part_p = call(
        peer_forward_kernel, "peer_forward", (rows_bf, hid_bf, hid_bf, rows_bf),
        2 * mm, 9 * MIB, (x_peer, gain, win, wout), small_o,
    )
    part_recv = swap(part_p)
    dpre_p, back_p, tail = call(
        peer_backward_kernel, "peer_backward", (hid_bf, shape((tok + TAIL, width), BF), shape((TAIL, width), BF)),
        2 * mm, 9 * MIB, (x_peer, db_peer, slope_p, part_p, small_o, gain, router, win, wout),
    )
    back_recv = swap(back_p)
    y_pack, mix_done = call(
        mix_kernel, "mix", (slots_bf, shape((8, 128), F32)), place_cost, 8 * MIB, (base_o, gate, part_recv, place)
    )
    half = hidden // 2
    left = pl.BlockSpec((tok, half), lambda i: (0, i))
    right = pl.BlockSpec((tok, width), lambda i: (0, 0))
    grad = pl.BlockSpec((half, width), lambda i: (i, 0))
    token = shape((8, 128), F32)
    gin, gout, grads_done = call(
        grads_kernel, "weight_grads", (shape((hidden, width), F32), shape((hidden, width), F32), token),
        LONG, 16 * MIB, (dpre_o, dpre_p, normed_o, normed_p, hid_o, hid_p, db_own, db_peer), mix_done,
        grid=(2,),
        in_specs=[left, left, right, right, left, left, right, right],
        out_specs=(grad, grad, pl.BlockSpec((8, 128), lambda i: (0, 0))),
    )
    y_buf = exchange(y_pack.reshape(experts, cap, width), experts).reshape(slots, width)
    back_pack, small = call(
        add_kernel, "add_back", (slots_bf, shape((2, width), F32)), place_cost, 5 * MIB,
        (back_o, tail, back_recv, place), grads_done, 24,
        in_specs=[inside, inside, outer, inside],
        out_specs=(outer, inside),
        scratch_shapes=[
            pltpu.VMEM((tok + TAIL, width), BF),
            pltpu.VMEM((slots, width), BF),
            pltpu.SemaphoreType.DMA((7,)),
        ],
    )
    back_pack, y_buf = lax.optimization_barrier((back_pack, y_buf))
    back_buf = exchange(back_pack.reshape(experts, cap, width), experts).reshape(slots, width)
    mixed, home = call(
        unpack_kernel, "unpack", (rows_bf, shape((tok, slots), BF)), place_cost, 4 * MIB, (slot, y_buf)
    )
    input_grad = call(
        unpack_last_kernel, "unpack_last", rows_bf, place_cost, 4 * MIB, (home, back_buf), None, 40,
        in_specs=[inside, outer],
        out_specs=outer,
        scratch_shapes=[
            pltpu.VMEM((slots, width), BF),
            pltpu.VMEM((tok, width), BF),
            pltpu.SemaphoreType.DMA((8,)),
        ],
    )
    return (mixed[None], input_grad[None], gin[None], gout[None], small[:1], small[1:])


def solution(mesh):
    return jax.shard_map(
        local,
        mesh=mesh,
        in_specs=(
            P("dp", "expert", None),
            P("dp", "expert", None),
            P("dp", "expert"),
            P("expert", None),
            P("expert", None),
            P("expert", "dp", None),
            P("expert", "dp", None),
        ),
        out_specs=(
            P("dp", "expert", None),
            P("dp", "expert", None),
            P("expert", "dp", None),
            P("expert", "dp", None),
            P("expert", None),
            P("expert", None),
        ),
        check_vma=False,
    )
```
